256 devices in a mesh: blk: 32 (over z, x_lo, core), cols: 8 (over y, x_hi).
Axes of the slice: x: 4 (x_hi: 2, x_lo: 2; x = x_hi * 2 + x_lo), y: 4, z: 8, core: 2. Of those that a mesh axis runs over, the one named last changes fastest.
Arguments:
- queries: bfloat16 [4096, 768], P('blk'), may hold values from -6 to 6
- label_ids: int32 [4096, 8], P('blk'), may hold values from -1 to 131071, as said below
- weights: float32 [131072, 768], P(('blk', 'cols')), may hold values from -0.21875 to 0.21875
- momentum: float32 [131072, 768], P(('blk', 'cols')), may hold values from -12 to 12
Outputs:
- new_weights: float32 [131072, 768], P(('blk', 'cols'))
- new_momentum: float32 [131072, 768], P(('blk', 'cols'))
- query_grad: float32 [4096, 768], P('blk')
The draws below stay inside these ranges and needn't reach their ends.
Inputs may be any that keep to these rules, and one draw needn't show every extreme that they name: `label_ids`: each query lists 1 to 8 label ids in its first entries and -1 in the rest; ids may repeat within a list; some query lists 8 ids and some lists one.
All inputs are finite; a program needn't handle non-finite values.
Results may differ from the reference program's by a relative error of at most 0.0027.
Values may be sent and summed in bfloat16 or wider, within the bound.
A program may use at most 128 MiB of HBM per device.

```python
import jax
import jax.numpy as jnp
from jax import lax

D = 768
LIST = 8
LAB_DEV = 512
TOKENS = 4096
LABELS = 131072


def draw_label_ids(key, part):
    key = jax.random.fold_in(key, 7)
    key_ids = jax.random.fold_in(key, 1)
    key_counts = jax.random.fold_in(key, 2)
    label_vals = jax.random.randint(key_ids, (TOKENS, LIST), 0, LABELS, dtype=jnp.int32)
    counts = jax.random.randint(key_counts, (TOKENS, 1), 1, LIST + 1, dtype=jnp.int32)
    row_iota = jnp.arange(TOKENS, dtype=jnp.int32)[:, None]
    counts = jnp.where(row_iota == 0, LIST, counts)
    counts = jnp.where(row_iota == 1, 1, counts)
    slot_iota = jnp.arange(LIST, dtype=jnp.int32)[None, :]
    label_vals = jnp.where((row_iota == 0) & (slot_iota == 0), LABELS - 1, label_vals)
    return jnp.where(slot_iota < counts, label_vals, -1).astype(jnp.int32)


def levels(rng, extent, shards, smallest, high):
    gain, own = 1.0, jax.random.fold_in(rng, 6)
    for position, shards_of in shards:
        steps = jnp.exp(jax.random.uniform(jax.random.fold_in(own, position), (shards_of,), jnp.float32, smallest / len(shards), high / len(shards)))
        gain = gain * jnp.repeat(steps, extent[position] // shards_of).reshape([-1 if axis == position else 1 for axis in range(len(extent))])
    return gain


def normal_values(key, extent, scale, reach, split=(), held_as=jnp.bfloat16):
    values = scale * jax.random.normal(key, extent, jnp.float32)
    if split:
        values = values * levels(key, extent, split, -0.22, 0.18)
    return jnp.clip(values, -reach, reach).astype(held_as)


def setup_inputs(seed: int = 0) -> dict:
    keys = jax.random.split(jax.random.key(seed), 5)
    queries = normal_values(keys[0], (TOKENS, D), 1.0, 6.0, ((0, 32),))
    label_ids = draw_label_ids(jax.random.fold_in(keys[4], 71), 0)
    weights = normal_values(keys[2], (LABELS, D), D ** -0.5, 0.21875, ((0, 256),), jnp.float32)
    momentum = normal_values(keys[3], (LABELS, D), 2.0, 12.0, ((0, 256),), jnp.float32)
    return dict(queries=queries, label_ids=label_ids, weights=weights, momentum=momentum)


loss_scale = 1.0 / 16.0
keep_rate = 0.9
step_rate = 0.005


def reference(queries, label_ids, weights, momentum):
    nblocks = LABELS // LAB_DEV
    w_blocks = weights.reshape(nblocks, LAB_DEV, D)
    m_blocks = momentum.reshape(nblocks, LAB_DEV, D)
    offsets = jnp.arange(nblocks, dtype=jnp.int32) * LAB_DEV
    lab_iota = jnp.arange(LAB_DEV, dtype=jnp.int32)

    def one_block(q_grad, item):
        w_rows, m_rows, offset = item
        w_half = w_rows.astype(jnp.bfloat16)
        scores = jnp.dot(queries, w_half.T, preferred_element_type=jnp.float32)
        local = (label_ids - offset).astype(jnp.int32)
        target = jnp.any(local[:, :, None] == lab_iota[None, None, :], axis=1).astype(jnp.float32)
        grad = ((jax.nn.sigmoid(scores) - target) * loss_scale).astype(jnp.bfloat16)
        w_grad = jnp.dot(grad.T, queries, preferred_element_type=jnp.float32)
        new_m = keep_rate * m_rows + w_grad
        new_w = w_rows - step_rate * new_m
        q_grad = q_grad + jnp.dot(grad, w_half, preferred_element_type=jnp.float32)
        return q_grad, (new_w, new_m)

    start = jnp.zeros((TOKENS, D), jnp.float32)
    q_grad, (new_w, new_m) = lax.scan(one_block, start, (w_blocks, m_blocks, offsets))
    return new_w.reshape(LABELS, D), new_m.reshape(LABELS, D), q_grad
```

```python
import functools

import jax
import jax.numpy as jnp
from jax import lax
from jax.experimental import pallas as pl
from jax.experimental.pallas import tpu as pltpu
from jax.sharding import PartitionSpec as P

MESH = pl.DeviceIdType.MESH
F32, BF16 = jnp.float32, jnp.bfloat16
NT = (((1,), (1,)), ((), ()))
TN = (((0,), (0,)), ((), ()))
NN = (((1,), (0,)), ((), ()))

loss_scale = 1.0 / 16.0
keep_rate = 0.9
step_rate = 0.005

D = 768
LAB = 512
QB = 128
ZN, YN, XN = 8, 4, 4
LIST = 8
SUB = 4
PIECE = LAB // 2 // SUB
PLACE = {1: 0, 7: 1, 2: 2, 6: 3, 3: 4, 5: 5, 4: 6, 0: 7}
QUARTER = QB // 4


def dot(a, b, dims):
    return lax.dot_general(a, b, dims, preferred_element_type=F32)


def device(z, y, x, core):
    return (z * 4 + (x % 2) * 2 + core, y * 2 + x // 2)


def copy_names():
    names = []
    for way in "+-":
        for step in range(1, 5):
            for quarter in range(2):
                if step < 4 or quarter == (0 if way == "+" else 1):
                    names.append(("zg", way, step, quarter))
            if step < 4 or way == "+":
                names.append(("id", way, step))
    names += [("yg", r, k) for r in range(1, 8) for k in range(2)]
    names += [("cw",)]
    names += [(kind, way, i) for kind in ("xw", "fw", "gc", "gx") for way in "+-" for i in range(SUB)]
    names += [("go", i) for i in range(2)]
    names += [("yr", r, k) for r in range(8) for k in range(2)]
    for way in "+-":
        for step in range(1, 5):
            for quarter in range(2):
                if step > 1 or quarter == (0 if way == "+" else 1):
                    names.append(("zr", way, step, quarter))
    names += [("rs", k) for k in range(1, 4)]
    names += [("ag", k) for k in range(1, 8)]
    return names


NAMES = {name: i for i, name in enumerate(copy_names())}


def kernel(
    q_in, ids_in, w_in, wg_out, qg_out,
    Q, IDS, M, WF, W, WG, QG, YS, YR, ZS, ZR, GOS, GOR, GCS, GCR, GXS, GXR, RS, RR, OUT, local_sem, send_sem, recv_sem,
):
    blk, cols = lax.axis_index("blk"), lax.axis_index("cols")
    z, xl, core = blk // 4, (blk // 2) % 2, blk % 2
    y, xh = cols // 2, cols % 2
    x = xh * 2 + xl
    p = y % 2

    z_of = {"+": device((z + 1) % ZN, y, x, core), "-": device((z + ZN - 1) % ZN, y, x, core)}
    y_of = {"+": device(z, (y + 1) % YN, x, core), "-": device(z, (y + YN - 1) % YN, x, core)}
    x_of = {"+": device(z, y, (x + 1) % XN, core), "-": device(z, y, (x + XN - 1) % XN, core)}
    partner = device(z, y, x, 1 - core)
    far_x = (x + 2) % XN
    same = {k: device(z, (y + k // 2) % YN, far_x if k % 2 else x, core) for k in range(1, 8)}

    cq = pltpu.make_async_copy(q_in, Q.at[pl.ds(PLACE[0] * QB, QB)], local_sem.at[0])
    cq.start()
    cw = pltpu.make_async_copy(w_in, WF, local_sem.at[1])
    cw.start()

    barrier = pltpu.get_barrier_semaphore()
    greeted = [partner] + [t[w] for t in (z_of, x_of) for w in "+-"] + list(same.values())
    for d in greeted:
        pl.semaphore_signal(barrier, inc=1, device_id=d, device_id_type=MESH)

    ids = ids_in[...]
    wide = jnp.concatenate([ids, jnp.zeros((QB, 128 - LIST), jnp.int32)], axis=1)
    IDS[0] = jnp.transpose(wide)[:LIST]

    cps = {}

    def start(name, src, dst, dev):
        cp = pltpu.make_async_remote_copy(
            src_ref=src, dst_ref=dst, send_sem=send_sem.at[NAMES[name]], recv_sem=recv_sem.at[NAMES[name]],
            device_id=dev, device_id_type=MESH,
        )
        cp.start()
        cps[name] = cp

    def arrived(*names):
        for name in names:
            cps[name].wait_recv()

    def rows(slot, half, quarter):
        return pl.ds(pl.multiple_of(PLACE[slot] * QB + half * (QB // 2) + quarter * QUARTER, QUARTER), QUARTER)

    def gather_z(way, step, quarter):
        src, dst = ((9 - step) % 8, 8 - step) if way == "+" else (step - 1, step)
        start(("zg", way, step, quarter), Q.at[rows(src, p, quarter)], Q.at[rows(dst, p, quarter)], z_of[way])

    def gather_ids(way, step):
        src, dst = ((9 - step) % 8, 8 - step) if way == "+" else (step - 1, step)
        start(("id", way, step), IDS.at[src], IDS.at[dst], z_of[way])

    def gather_y(slot, quarter):
        here = Q.at[rows(slot, p, quarter)]
        start(("yg", slot, quarter), here, here, y_of["+-"[quarter]])

    def step_gather(step):
        for quarter in range(2):
            for way in "+-":
                if ("zg", way, step, quarter) not in NAMES:
                    continue
                arrived(("zg", way, step, quarter))
                if ("zg", way, step + 1, quarter) in NAMES:
                    gather_z(way, step + 1, quarter)
                gather_y(8 - step if way == "+" else step, quarter)
        for way in "+-":
            if ("id", way, step) in NAMES:
                arrived(("id", way, step))
                if ("id", way, step + 1) in NAMES:
                    gather_ids(way, step + 1)

    def forward_weights(i):
        for way, base in (("+", 2 * LAB), ("-", 3 * LAB)):
            arrived(("xw", way, i))
            start(("fw", way, i), W.at[pl.ds(base + i * PIECE, PIECE)],
                  W.at[pl.ds(base + LAB // 2 + i * PIECE, PIECE)], partner)

    def first(z, y, x, core):
        b, c = device(z, y, x, core)
        return (b * 8 + c) * LAB

    left, right = (x + XN - 1) % XN, (x + 1) % XN
    half = LAB // 2
    pieces = [
        (0, LAB, first(z, y, x, core)),
        (LAB, LAB, first(z, y, x, 1 - core)),
        (2 * LAB, half, first(z, y, left, core) + half),
        (2 * LAB + half, half, first(z, y, left, 1 - core) + half),
        (3 * LAB, half, first(z, y, right, core)),
        (3 * LAB + half, half, first(z, y, right, 1 - core)),
    ]

    def build_mask(slot):
        ids = IDS[slot]
        row = jnp.full(ids.shape, -1, jnp.int32)
        for base, count, label in pieces:
            local = ids - label
            row = jnp.where((local >= 0) & (local < count), local + base, row)
        low = jnp.where(row >= 0, row % 128, -1)
        bit = jnp.left_shift(1, jnp.maximum(row, 0) // 128)
        sub = lax.broadcasted_iota(jnp.int32, (128, QB), 0)
        m = jnp.zeros((128, QB), jnp.int32)
        for j in range(LIST):
            m = m | jnp.where(low[j:j + 1] == sub, bit[j:j + 1], 0)
        M[PLACE[slot] * QB:(PLACE[slot] + 1) * QB] = jnp.transpose(m)

    seen = set()

    def work(slot, part):
        at = PLACE[slot] * QB
        here, there = slice(at, at + 2 * QB), slice(part * 2 * LAB, (part + 1) * 2 * LAB)
        q, w, m = Q[here], W[there], M[here]
        scores = dot(q, w, NT)
        out = []
        for b in range(2 * LAB // 128):
            target = ((m >> (part * 2 * LAB // 128 + b)) & 1).astype(F32)
            out.append(((jax.nn.sigmoid(scores[:, b * 128:(b + 1) * 128]) - target) * loss_scale).astype(BF16))
        grad = jnp.concatenate(out, axis=1)
        a = dot(grad, w, NN)
        if part == 0:
            QG[here] = a
        else:
            QG[here] += a
        g = dot(grad, q, TN)
        if part not in seen:
            WG[there] = g
        else:
            WG[there] += g
        seen.add(part)

    def reduce_y(slot):
        for k in range(2):
            YS[slot, k] = QG[rows(slot, 1 - p, k)].astype(BF16)
            start(("yr", slot, k), YS.at[slot, k], YR.at[slot, k], y_of["-+"[k]])

    def total(slot, quarter):
        arrived(("yr", slot, quarter))
        t = QG[rows(slot, p, quarter)] + YR[slot, quarter].astype(F32)
        for i, way in enumerate("+-"):
            step = 4 - slot if way == "+" else (slot - 4 if slot else 4)
            if ("zr", way, step, quarter) in NAMES and (slot == 0 or (slot < 4) == (way == "+")):
                arrived(("zr", way, step, quarter))
                t = t + ZR[i, step - 1, quarter].astype(F32)
        return t

    def reduce_z(step):
        for quarter in range(2):
            for i, way in enumerate("+-"):
                if ("zr", way, step, quarter) not in NAMES:
                    continue
                slot = 5 - step if way == "+" else 3 + step
                ZS[i, step - 1, quarter] = total(slot, quarter).astype(BF16)
                start(("zr", way, step, quarter), ZS.at[i, step - 1, quarter], ZR.at[i, step - 1, quarter], z_of[way])

    cq.wait()
    pl.semaphore_wait(barrier, len(greeted))
    for quarter in range(2):
        for way in "+-":
            gather_z(way, 1, quarter)
    for way in "+-":
        gather_ids(way, 1)
    cw.wait()
    W[:LAB] = WF[...].astype(BF16)
    start(("cw",), W.at[pl.ds(0, LAB)], W.at[pl.ds(LAB, LAB)], partner)
    for i in range(SUB):
        start(("xw", "+", i), W.at[pl.ds(half + i * PIECE, PIECE)], W.at[pl.ds(2 * LAB + i * PIECE, PIECE)], x_of["+"])
        start(("xw", "-", i), W.at[pl.ds(i * PIECE, PIECE)], W.at[pl.ds(3 * LAB + i * PIECE, PIECE)], x_of["-"])
    build_mask(0)

    step_gather(1)
    build_mask(1)
    build_mask(7)
    forward_weights(0)
    step_gather(2)
    build_mask(2)
    build_mask(6)
    arrived(("cw",), *[("yg", s, k) for s in (1, 7) for k in range(2)])
    work(1, 0)
    forward_weights(1)
    step_gather(3)
    build_mask(3)
    build_mask(5)
    arrived(*[("yg", s, k) for s in (2, 6) for k in range(2)])
    work(2, 0)
    forward_weights(2)
    step_gather(4)
    build_mask(4)
    forward_weights(3)
    arrived(*[("yg", s, k) for s in (3, 5) for k in range(2)])
    work(3, 0)
    arrived(*[("yg", 4, k) for k in range(2)])
    work(4, 0)
    arrived(*[("fw", way, i) for way in "+-" for i in range(SUB)])
    work(4, 1)
    reduce_y(4)
    work(3, 1)
    reduce_y(3)
    reduce_y(5)
    reduce_z(1)
    work(2, 1)
    reduce_y(2)
    reduce_y(6)
    reduce_z(2)
    work(1, 1)
    reduce_y(1)
    reduce_y(7)
    reduce_y(0)

    for n, (way, base) in enumerate((("+", 2 * LAB), ("-", 3 * LAB))):
        for i in range(SUB):
            GCS[n, i] = WG[base + half + i * PIECE:base + half + (i + 1) * PIECE].astype(BF16)
            start(("gc", way, i), GCS.at[n, i], GCR.at[n, i], partner)
    for i in range(2):
        GOS[i] = WG[LAB + i * half:LAB + (i + 1) * half].astype(BF16)
        start(("go", i), GOS.at[i], GOR.at[i], partner)
    reduce_z(3)
    for i in range(SUB):
        for n, (way, base) in enumerate((("+", 2 * LAB), ("-", 3 * LAB))):
            arrived(("gc", way, i))
            GXS[n, i] = (WG[base + i * PIECE:base + (i + 1) * PIECE] + GCR[n, i].astype(F32)).astype(BF16)
            start(("gx", way, i), GXS.at[n, i], GXR.at[n, i], x_of["-" if way == "+" else "+"])
    reduce_z(4)
    for i in range(2):
        arrived(("go", i))
        WG[i * half:(i + 1) * half] += GOR[i].astype(F32)

    ry, rx = y // 2, xh
    mine = ry * 2 + rx
    done = {}
    sums = [total(0, quarter) for quarter in range(2)]
    for quarter in range(2):
        RS[quarter * QUARTER:(quarter + 1) * QUARTER] = sums[quarter]
    eighth = QB // 8
    for k in range(1, 4):
        owner = ((ry + k // 2) % 2) * 2 + (rx + k) % 2
        take = pl.ds(pl.multiple_of(owner * eighth, eighth), eighth)
        RR[0, k] = RS[take].astype(BF16)
        start(("rs", k), RR.at[0, k], RR.at[1, k], same[2 * (k // 2) * 2 + k % 2])
    for i in range(SUB):
        for n, (way, base) in enumerate((("+", half), ("-", 0))):
            arrived(("gx", way, i))
            wg_out[base + i * PIECE:base + (i + 1) * PIECE] = (
                WG[base + i * PIECE:base + (i + 1) * PIECE] + GXR[n, i].astype(F32)
            )
    t = RS[pl.ds(pl.multiple_of(mine * eighth, eighth), eighth)]
    for k in range(1, 4):
        arrived(("rs", k))
        t = t + RR[1, k].astype(F32)
    place = pl.ds(pl.multiple_of(p * (QB // 2) + mine * eighth, eighth), eighth)
    OUT[place] = t.astype(BF16)
    for k in range(1, 8):
        start(("ag", k), OUT.at[place], OUT.at[place], same[k])
    for k in range(1, 8):
        arrived(("ag", k))
    qg_out[...] = OUT[...]
    for cp in cps.values():
        cp.wait_send()


def step(queries, label_ids, weights):
    n = len(NAMES)
    vmem = pl.BlockSpec(memory_space=pltpu.VMEM)
    anywhere = pl.BlockSpec(memory_space=pl.ANY)
    tokens = ZN * QB
    labels = 4 * LAB
    return pl.pallas_call(
        kernel,
        out_shape=(jax.ShapeDtypeStruct((LAB, D), F32), jax.ShapeDtypeStruct((QB, D), BF16)),
        in_specs=[anywhere, vmem, anywhere],
        out_specs=(vmem, vmem),
        scratch_shapes=[
            pltpu.VMEM((tokens, D), BF16),
            pltpu.VMEM((8, LIST, QB), jnp.int32),
            pltpu.VMEM((tokens, 128), jnp.int32),
            pltpu.VMEM((LAB, D), F32),
            pltpu.VMEM((labels, D), BF16),
            pltpu.VMEM((labels, D), F32),
            pltpu.VMEM((tokens, D), F32),
            pltpu.VMEM((8, 2, QUARTER, D), BF16),
            pltpu.VMEM((8, 2, QUARTER, D), BF16),
            pltpu.VMEM((2, 4, 2, QUARTER, D), BF16),
            pltpu.VMEM((2, 4, 2, QUARTER, D), BF16),
            pltpu.VMEM((2, LAB // 2, D), BF16),
            pltpu.VMEM((2, LAB // 2, D), BF16),
            pltpu.VMEM((2, SUB, PIECE, D), BF16),
            pltpu.VMEM((2, SUB, PIECE, D), BF16),
            pltpu.VMEM((2, SUB, PIECE, D), BF16),
            pltpu.VMEM((2, SUB, PIECE, D), BF16),
            pltpu.VMEM((QB // 2, D), F32),
            pltpu.VMEM((2, 4, QB // 8, D), BF16),
            pltpu.VMEM((QB, D), BF16),
            pltpu.SemaphoreType.DMA((2,)),
            pltpu.SemaphoreType.DMA((n,)),
            pltpu.SemaphoreType.DMA((n,)),
        ],
        compiler_params=pltpu.CompilerParams(
            collective_id=0, has_side_effects=True, vmem_limit_bytes=56 * 1024 * 1024
        ),
        name="step",
    )(queries, label_ids, weights)


def body(queries, label_ids, weights, momentum):
    w_grad, q_grad = step(queries, label_ids, weights)
    new_momentum = keep_rate * momentum + w_grad
    new_weights = weights - step_rate * new_momentum
    return new_weights, new_momentum, q_grad.astype(F32)


def solution(mesh):
    return jax.shard_map(
        body,
        mesh=mesh,
        in_specs=(P("blk", None), P("blk", None), P(("blk", "cols"), None), P(("blk", "cols"), None)),
        out_specs=(P(("blk", "cols"), None), P(("blk", "cols"), None), P("blk", None)),
        check_vma=False,
    )
```

```python
import functools

import jax
import jax.numpy as jnp
from jax import lax
from jax.experimental import pallas as pl
from jax.experimental.pallas import tpu as pltpu
from jax.sharding import PartitionSpec as P

MESH = pl.DeviceIdType.MESH
F32, BF16 = jnp.float32, jnp.bfloat16
NT = (((1,), (1,)), ((), ()))
TN = (((0,), (0,)), ((), ()))
NN = (((1,), (0,)), ((), ()))

loss_scale = 1.0 / 16.0
keep_rate = 0.9
step_rate = 0.005

D = 768
LAB = 512
QB = 128
ZN, YN, XN = 8, 4, 4
LIST = 8
SUB = 4
PIECE = LAB // 2 // SUB
PLACE = {1: 0, 7: 1, 2: 2, 6: 3, 3: 4, 5: 5, 4: 6, 0: 7}
QUARTER = QB // 4


def dot(a, b, dims):
    return lax.dot_general(a, b, dims, preferred_element_type=F32)


def device(z, y, x, core):
    return (z * 4 + (x % 2) * 2 + core, y * 2 + x // 2)


TOWARDS = {3: 2, 2: 1, 1: 0, 5: 6, 6: 7, 7: 0}
PARTS = {slot: 3 if slot == 4 else 2 for slot in range(8)}


def copy_names():
    names = [("zg", r, k) for r in range(1, 8) for k in range(2)] + [("id", r) for r in range(1, 8)]
    names += [("yg", r, k) for r in range(1, 8) for k in range(2)]
    names += [("cw",)]
    names += [(kind, way, i) for kind in ("xw", "fw", "gc", "gx") for way in "+-" for i in range(SUB)]
    names += [("go", i) for i in range(2)]
    names += [("yr", r, k) for r in range(8) for k in range(PARTS[r])]
    names += [("zr", r, k) for r in (3, 2, 5, 6) for k in range(2)]
    names += [("zl", r, m) for r in (0, 1, 7, 4) for m in range(2 if r == 4 else 4) if r or m]
    names += [("ag", k) for k in range(1, 8)]
    return names


NAMES = {name: i for i, name in enumerate(copy_names())}


def kernel(
    q_in, ids_in, w_in, wg_out, qg_out,
    Q, IDS, M, WF, W, WG, QG, YS, YR, ZS, ZR, GOS, GOR, GCS, GCR, GXS, GXR, LS, LR, OWN, OUT, local_sem, send_sem, recv_sem,
):
    blk, cols = lax.axis_index("blk"), lax.axis_index("cols")
    z, xl, core = blk // 4, (blk // 2) % 2, blk % 2
    y, xh = cols // 2, cols % 2
    x = xh * 2 + xl
    p = y % 2

    s = y // 2
    z_of = {r: device((z + r) % ZN, y, x, core) for r in range(1, 8)}
    y_of = {k: device(z, (y + k) % YN, x, core) for k in (1, 2, 3)}
    x_of = {"+": device(z, y, (x + 1) % XN, core), "-": device(z, y, (x + XN - 1) % XN, core)}
    partner = device(z, y, x, 1 - core)
    far_x = (x + 2) % XN
    same = {k: device(z, (y + k // 2) % YN, far_x if k % 2 else x, core) for k in range(1, 8)}

    cq = pltpu.make_async_copy(q_in, Q.at[pl.ds(PLACE[0] * QB, QB)], local_sem.at[0])
    cq.start()
    cw = pltpu.make_async_copy(w_in, WF, local_sem.at[1])
    cw.start()

    barrier = pltpu.get_barrier_semaphore()
    def owner(r, m):
        return device((z + r) % ZN, (y + 2 * (m // 2)) % YN, far_x if m % 2 else x, core)

    greeted = [partner] + list(x_of.values()) + list(same.values())
    greeted += [owner(r, m) for r in (1, 7) for m in range(4)] + [owner(4, 0), owner(4, 1)]
    for d in greeted:
        pl.semaphore_signal(barrier, inc=1, device_id=d, device_id_type=MESH)

    IDS[0] = ids_in[...]

    cps = {}

    def start(name, src, dst, dev):
        cp = pltpu.make_async_remote_copy(
            src_ref=src, dst_ref=dst, send_sem=send_sem.at[NAMES[name]], recv_sem=recv_sem.at[NAMES[name]],
            device_id=dev, device_id_type=MESH,
        )
        cp.start()
        cps[name] = cp

    def arrived(*names):
        for name in names:
            cps[name].wait_recv()

    def rows(slot, half, quarter, count=QUARTER):
        return pl.ds(pl.multiple_of(PLACE[slot] * QB + half * (QB // 2) + quarter * QUARTER, QUARTER), count)

    def gather_z(slot, k, src):
        start(("zg", slot, k), Q.at[rows(src, p, k)], Q.at[rows(slot, p, k)], z_of[7 if src < 4 and slot == src + 1 else 1])

    def gather_ids(slot):
        src = TOWARDS[slot]
        if src:
            arrived(("id", src))
        start(("id", slot), IDS.at[src], IDS.at[slot], z_of[7 if slot < 4 else 1])

    def gather_step(step, k):
        for slot in (8 - step, step) if step < 4 else (4,):
            arrived(("zg", slot, k))
            if step < 3:
                gather_z(slot - 1 if slot > 4 else slot + 1, k, slot)
            elif step == 3 and slot == (5, 3)[k]:
                gather_z(4, k, slot)
            here = Q.at[rows(slot, p, k)]
            start(("yg", slot, k), here, here, y_of[1 + 2 * k])

    def gathered(*slots):
        for slot in slots:
            arrived(("yg", slot, 0), ("yg", slot, 1))

    def forward_weights(i):
        for way, base in (("+", 2 * LAB), ("-", 3 * LAB)):
            arrived(("xw", way, i))
            start(("fw", way, i), W.at[pl.ds(base + i * PIECE, PIECE)],
                  W.at[pl.ds(base + LAB // 2 + i * PIECE, PIECE)], partner)

    def first(z, y, x, core):
        b, c = device(z, y, x, core)
        return (b * 8 + c) * LAB

    left, right = (x + XN - 1) % XN, (x + 1) % XN
    half = LAB // 2
    pieces = [
        (0, LAB, first(z, y, x, core)),
        (LAB, LAB, first(z, y, x, 1 - core)),
        (2 * LAB, half, first(z, y, left, core) + half),
        (2 * LAB + half, half, first(z, y, left, 1 - core) + half),
        (3 * LAB, half, first(z, y, right, core)),
        (3 * LAB + half, half, first(z, y, right, 1 - core)),
    ]

    def build_mask(slot):
        ids = IDS[slot]
        row = jnp.full(ids.shape, -1, jnp.int32)
        for base, count, label in pieces:
            local = ids - label
            row = jnp.where((local >= 0) & (local < count), local + base, row)
        low = jnp.where(row >= 0, row % 128, -1)
        bit = jnp.left_shift(1, jnp.maximum(row, 0) // 128)
        sub = lax.broadcasted_iota(jnp.int32, (128, QB), 0)
        m = jnp.zeros((128, QB), jnp.int32)
        for j in range(LIST):
            m = m | jnp.where(low[j:j + 1] == sub, bit[j:j + 1], 0)
        M[PLACE[slot] * QB:(PLACE[slot] + 1) * QB] = jnp.transpose(m)

    seen = set()

    def work(slot, part):
        at = PLACE[slot] * QB
        here, there = slice(at, at + 2 * QB), slice(part * 2 * LAB, (part + 1) * 2 * LAB)
        q, w, m = Q[here], W[there], M[here]
        scores = dot(q, w, NT)
        out = []
        for b in range(2 * LAB // 128):
            target = ((m >> (part * 2 * LAB // 128 + b)) & 1).astype(F32)
            out.append(((jax.nn.sigmoid(scores[:, b * 128:(b + 1) * 128]) - target) * loss_scale).astype(BF16))
        grad = jnp.concatenate(out, axis=1)
        a = dot(grad, w, NN)
        if (slot,) not in seen:
            QG[here] = a
        else:
            QG[here] += a
        g = dot(grad, q, TN)
        if part not in seen:
            WG[there] = g
        else:
            WG[there] += g
        seen.update([part, (slot,)])

    def reduce_y(slot):
        for k in range(PARTS[slot]):
            if slot == 4:
                there = (y + k + 1) % YN
                YS[slot, k] = QG[rows(slot, there % 2, there // 2)].astype(BF16)
                start(("yr", slot, k), YS.at[slot, k], YR.at[slot, k], y_of[k + 1])
            else:
                YS[slot, k] = QG[rows(slot, 1 - p, k)].astype(BF16)
                start(("yr", slot, k), YS.at[slot, k], YR.at[slot, k], y_of[3 - 2 * k])

    def eighth(which):
        return pl.ds(pl.multiple_of(which * (QB // 8), QB // 8), QB // 8)

    def total(slot, k):
        arrived(("yr", slot, k))
        t = QG[rows(slot, p, k)] + YR[slot, k].astype(F32)
        before = {2: 3, 1: 2, 6: 5, 7: 6}.get(slot)
        if before:
            arrived(("zr", before, k))
            t = t + ZR[slot, k].astype(F32)
        return t

    def reduce_z(slot):
        for k in range(2):
            ZS[slot, k] = total(slot, k).astype(BF16)
            start(("zr", slot, k), ZS.at[slot, k], ZR.at[TOWARDS[slot], k], z_of[1 if slot < 4 else 7])

    def reduce_last(slot):
        if slot == 4:
            arrived(*[("yr", 4, k) for k in range(3)])
            t = QG[rows(4, p, s)]
            for k in range(3):
                t = t + YR[4, k].astype(F32)
            LS[4, :QUARTER] = t.astype(BF16)
        else:
            for k in range(2):
                t = total(slot, k)
                LS[slot, k * QUARTER:(k + 1) * QUARTER] = t.astype(BF16)
                if slot == 0:
                    OWN[k * QUARTER:(k + 1) * QUARTER] = t
        for m in range(4):
            if ("zl", slot, m) in NAMES:
                j = (xh + m) % 2
                part = eighth(j if slot == 4 else (s + m // 2) % 2 * 2 + j)
                start(("zl", slot, m), LS.at[slot, part], LR.at[slot, m], owner(slot, m))

    cq.wait()
    pl.semaphore_wait(barrier, len(greeted))
    for slot in (7, 1):
        gather_z(slot, 0, 0)
    gather_ids(1)
    gather_ids(7)
    start(("id", 4), IDS.at[0], IDS.at[4], z_of[4])
    cw.wait()
    W[:LAB] = WF[...].astype(BF16)
    for slot in (7, 1):
        gather_z(slot, 1, 0)
    start(("cw",), W.at[pl.ds(0, LAB)], W.at[pl.ds(LAB, LAB)], partner)
    for i in range(SUB):
        start(("xw", "+", i), W.at[pl.ds(half + i * PIECE, PIECE)], W.at[pl.ds(2 * LAB + i * PIECE, PIECE)], x_of["+"])
        start(("xw", "-", i), W.at[pl.ds(i * PIECE, PIECE)], W.at[pl.ds(3 * LAB + i * PIECE, PIECE)], x_of["-"])
    build_mask(0)
    gather_step(1, 0)
    gather_ids(2)
    gather_ids(6)
    gather_step(1, 1)
    build_mask(1)
    build_mask(7)
    gather_step(2, 0)
    forward_weights(0)
    gather_ids(3)
    gather_ids(5)
    gather_step(2, 1)
    arrived(("cw",))
    gathered(1, 7)
    work(1, 0)
    gather_step(3, 0)
    forward_weights(1)
    build_mask(2)
    build_mask(6)
    gather_step(3, 1)
    forward_weights(2)
    arrived(("id", 4), ("id", 3), ("id", 5))
    gathered(2, 6)
    work(2, 0)
    forward_weights(3)
    gather_step(4, 0)
    gather_step(4, 1)
    for slot in (3, 5, 4):
        build_mask(slot)
    gathered(3, 5)
    work(3, 0)
    arrived(*[("fw", way, i) for way in "+-" for i in range(SUB)])
    work(3, 1)
    reduce_y(3)
    reduce_y(5)
    gathered(4)
    work(4, 0)
    work(4, 1)
    reduce_y(4)
    reduce_y(0)
    reduce_z(3)
    reduce_z(5)
    work(2, 1)
    reduce_y(2)
    reduce_y(6)
    reduce_last(4)
    reduce_last(0)
    work(1, 1)
    reduce_y(1)
    reduce_y(7)
    for n, (way, base) in enumerate((("+", 2 * LAB), ("-", 3 * LAB))):
        for i in range(SUB):
            GCS[n, i] = WG[base + half + i * PIECE:base + half + (i + 1) * PIECE].astype(BF16)
            start(("gc", way, i), GCS.at[n, i], GCR.at[n, i], partner)
    reduce_z(2)
    reduce_z(6)
    for i in range(SUB):
        for n, (way, base) in enumerate((("+", 2 * LAB), ("-", 3 * LAB))):
            arrived(("gc", way, i))
            GXS[n, i] = (WG[base + i * PIECE:base + (i + 1) * PIECE] + GCR[n, i].astype(F32)).astype(BF16)
            start(("gx", way, i), GXS.at[n, i], GXR.at[n, i], x_of["-" if way == "+" else "+"])
    for i in range(2):
        GOS[i] = WG[LAB + i * half:LAB + (i + 1) * half].astype(BF16)
        start(("go", i), GOS.at[i], GOR.at[i], partner)
    reduce_last(1)
    reduce_last(7)
    for i in range(2):
        arrived(("go", i))
        WG[i * half:(i + 1) * half] += GOR[i].astype(F32)

    t = OWN[eighth(s * 2 + xh)]
    for slot in (4, 0, 1, 7):
        for m in range(4):
            if ("zl", slot, m) in NAMES:
                arrived(("zl", slot, m))
                t = t + LR[slot, m].astype(F32)
    place = eighth(p * 4 + s * 2 + xh)
    OUT[place] = t.astype(BF16)
    for k in range(1, 8):
        start(("ag", k), OUT.at[place], OUT.at[place], same[k])
    for i in range(SUB):
        for n, (way, base) in enumerate((("+", half), ("-", 0))):
            arrived(("gx", way, i))
            wg_out[base + i * PIECE:base + (i + 1) * PIECE] = (
                WG[base + i * PIECE:base + (i + 1) * PIECE] + GXR[n, i].astype(F32)
            )
    for k in range(1, 8):
        arrived(("ag", k))
    qg_out[...] = OUT[...]
    for cp in cps.values():
        cp.wait_send()


def step(queries, label_ids, weights):
    n = len(NAMES)
    vmem = pl.BlockSpec(memory_space=pltpu.VMEM)
    anywhere = pl.BlockSpec(memory_space=pl.ANY)
    tokens = ZN * QB
    labels = 4 * LAB
    return pl.pallas_call(
        kernel,
        out_shape=(jax.ShapeDtypeStruct((LAB, D), F32), jax.ShapeDtypeStruct((QB, D), BF16)),
        in_specs=[anywhere, vmem, anywhere],
        out_specs=(vmem, vmem),
        scratch_shapes=[
            pltpu.VMEM((tokens, D), BF16),
            pltpu.VMEM((8, LIST, QB), jnp.int32),
            pltpu.VMEM((tokens, 128), jnp.int32),
            pltpu.VMEM((LAB, D), F32),
            pltpu.VMEM((labels, D), BF16),
            pltpu.VMEM((labels, D), F32),
            pltpu.VMEM((tokens, D), F32),
            pltpu.VMEM((8, 3, QUARTER, D), BF16),
            pltpu.VMEM((8, 3, QUARTER, D), BF16),
            pltpu.VMEM((8, 2, QUARTER, D), BF16),
            pltpu.VMEM((8, 2, QUARTER, D), BF16),
            pltpu.VMEM((2, LAB // 2, D), BF16),
            pltpu.VMEM((2, LAB // 2, D), BF16),
            pltpu.VMEM((2, SUB, PIECE, D), BF16),
            pltpu.VMEM((2, SUB, PIECE, D), BF16),
            pltpu.VMEM((2, SUB, PIECE, D), BF16),
            pltpu.VMEM((2, SUB, PIECE, D), BF16),
            pltpu.VMEM((8, QB // 2, D), BF16),
            pltpu.VMEM((8, 4, QB // 8, D), BF16),
            pltpu.VMEM((QB // 2, D), F32),
            pltpu.VMEM((QB, D), BF16),
            pltpu.SemaphoreType.DMA((2,)),
            pltpu.SemaphoreType.DMA((n,)),
            pltpu.SemaphoreType.DMA((n,)),
        ],
        compiler_params=pltpu.CompilerParams(
            collective_id=0, has_side_effects=True, vmem_limit_bytes=40 * 1024 * 1024
        ),
        name="step",
    )(queries, label_ids, weights)


def body(queries, label_ids, weights, momentum):
    w_grad, q_grad = step(queries, label_ids.T, weights)
    new_momentum = keep_rate * momentum + w_grad
    new_weights = weights - step_rate * new_momentum
    return new_weights, new_momentum, q_grad.astype(F32)


def solution(mesh):
    return jax.shard_map(
        body,
        mesh=mesh,
        in_specs=(P("blk", None), P("blk", None), P(("blk", "cols"), None), P(("blk", "cols"), None)),
        out_specs=(P(("blk", "cols"), None), P(("blk", "cols"), None), P("blk", None)),
        check_vma=False,
    )
```

```python
import functools

import jax
import jax.numpy as jnp
from jax import lax
from jax.experimental import pallas as pl
from jax.experimental.pallas import tpu as pltpu
from jax.sharding import PartitionSpec as P

MESH = pl.DeviceIdType.MESH
F32, BF16 = jnp.float32, jnp.bfloat16
NT = (((1,), (1,)), ((), ()))
TN = (((0,), (0,)), ((), ()))
NN = (((1,), (0,)), ((), ()))

loss_scale = 1.0 / 16.0
keep_rate = 0.9
step_rate = 0.005

D = 768
LAB = 512
QB = 128
ZN, YN, XN = 8, 4, 4
LIST = 8
SUB = 4
PIECE = LAB // 2 // SUB
PLACE = {1: 0, 7: 1, 2: 2, 6: 3, 3: 4, 5: 5, 4: 6, 0: 7}
QUARTER = QB // 4


def dot(a, b, dims):
    return lax.dot_general(a, b, dims, preferred_element_type=F32)


def device(z, y, x, core):
    return (z * 4 + (x % 2) * 2 + core, y * 2 + x // 2)


TOWARDS = {3: 2, 2: 1, 1: 0, 5: 6, 6: 7, 7: 0}
PARTS = {slot: 3 if slot == 4 else 2 for slot in range(8)}


def copy_names():
    names = [("zg", r, k) for r in range(1, 8) for k in range(2)] + [("id", r) for r in range(1, 8)]
    names += [("yg", r, k) for r in range(1, 8) for k in range(2)]
    names += [("cw",)]
    names += [(kind, way, i) for kind in ("xw", "fw", "gc", "gx") for way in "+-" for i in range(SUB)]
    names += [("go", i) for i in range(2)]
    names += [("yr", r, k) for r in range(8) for k in range(PARTS[r])]
    names += [("zr", r, k) for r in (3, 2, 5, 6) for k in range(2)]
    names += [("zl", r, m) for r in (0, 1, 7, 4) for m in range(2 if r == 4 else 4) if r or m]
    names += [("ag", k) for k in range(1, 8)]
    return names


NAMES = copy_names()
ROWS = {"zg": QUARTER, "yg": QUARTER, "cw": LAB, "xw": PIECE, "fw": PIECE, "gc": PIECE, "gx": PIECE, "go": LAB // 2,
        "yr": QUARTER, "zr": QUARTER, "zl": QB // 8, "ag": QB // 8, "id": 0}


def group(name):
    if name[0] in ("fw", "ag"):
        return name[:1]
    if name[0] in ("yg", "zl") or name[:2] == ("yr", 4):
        return name[:2]
    return name


GROUPS = list(dict.fromkeys(group(name) for name in NAMES))
KINDS = list(ROWS)


def kernel(
    q_in, ids_in, w_in, wg_out, qg_out,
    Q, IDS, M, WF, W, WG, QG, YS, YR, ZS, ZR, GOS, GOR, GCS, GCR, GXS, GXR, LS, LR, OWN, OUT, local_sem, send_sem, recv_sem,
):
    blk, cols = lax.axis_index("blk"), lax.axis_index("cols")
    z, xl, core = blk // 4, (blk // 2) % 2, blk % 2
    y, xh = cols // 2, cols % 2
    x = xh * 2 + xl
    p = y % 2

    s = y // 2
    z_of = {r: device((z + r) % ZN, y, x, core) for r in range(1, 8)}
    y_of = {k: device(z, (y + k) % YN, x, core) for k in (1, 2, 3)}
    x_of = {"+": device(z, y, (x + 1) % XN, core), "-": device(z, y, (x + XN - 1) % XN, core)}
    partner = device(z, y, x, 1 - core)
    far_x = (x + 2) % XN
    same = {k: device(z, (y + k // 2) % YN, far_x if k % 2 else x, core) for k in range(1, 8)}

    cq = pltpu.make_async_copy(q_in, Q.at[pl.ds(PLACE[0] * QB, QB)], local_sem.at[0])
    cq.start()
    ci = pltpu.make_async_copy(ids_in, IDS.at[0], local_sem.at[2])
    ci.start()
    cw = pltpu.make_async_copy(w_in, WF, local_sem.at[1])
    cw.start()

    barrier = pltpu.get_barrier_semaphore()
    def owner(r, m):
        return device((z + r) % ZN, (y + 2 * (m // 2)) % YN, far_x if m % 2 else x, core)

    greeted = [partner] + list(x_of.values()) + list(same.values())
    greeted += [owner(r, m) for r in (1, 7) for m in range(4)] + [owner(4, 0), owner(4, 1)]
    for d in greeted:
        pl.semaphore_signal(barrier, inc=1, device_id=d, device_id_type=MESH)


    started, waited = [], set()

    def start(name, src, dst, dev):
        pltpu.make_async_remote_copy(
            src_ref=src, dst_ref=dst, send_sem=send_sem.at[KINDS.index(name[0])],
            recv_sem=recv_sem.at[GROUPS.index(group(name))], device_id=dev, device_id_type=MESH,
        ).start()
        started.append(name)

    def await_bytes(names, index, sent):
        if names[0][0] == "id":
            ref = IDS.at[pl.ds(0, len(names))]
        else:
            ref = W.at[pl.ds(0, sum(ROWS[name[0]] for name in names))]
        cp = pltpu.make_async_remote_copy(
            src_ref=ref, dst_ref=ref, send_sem=send_sem.at[index if sent else 0], recv_sem=recv_sem.at[0 if sent else index],
            device_id=partner, device_id_type=MESH,
        )
        if sent:
            cp.wait_send()
        else:
            cp.wait_recv()

    def arrived(*names):
        for key in dict.fromkeys(group(name) for name in names):
            if key not in waited:
                waited.add(key)
                await_bytes([name for name in NAMES if group(name) == key], GROUPS.index(key), False)

    def sent(*kinds):
        for kind in kinds:
            await_bytes([name for name in started if name[0] == kind], KINDS.index(kind), True)

    def rows(slot, half, quarter, count=QUARTER):
        return pl.ds(pl.multiple_of(PLACE[slot] * QB + half * (QB // 2) + quarter * QUARTER, QUARTER), count)

    def gather_z(slot, k, src):
        start(("zg", slot, k), Q.at[rows(src, p, k)], Q.at[rows(slot, p, k)], z_of[7 if src < 4 and slot == src + 1 else 1])

    def gather_ids(slot):
        src = TOWARDS[slot]
        if src:
            arrived(("id", src))
        start(("id", slot), IDS.at[src], IDS.at[slot], z_of[7 if slot < 4 else 1])

    def gather_step(step, k):
        for slot in (8 - step, step) if step < 4 else (4,):
            arrived(("zg", slot, k))
            if step < 3:
                gather_z(slot - 1 if slot > 4 else slot + 1, k, slot)
            elif step == 3 and slot == (5, 3)[k]:
                gather_z(4, k, slot)
            here = Q.at[rows(slot, p, k)]
            start(("yg", slot, k), here, here, y_of[1 + 2 * k])

    def gathered(*slots):
        for slot in slots:
            arrived(("yg", slot, 0), ("yg", slot, 1))

    def forward_weights(i):
        for way, base in (("+", 2 * LAB), ("-", 3 * LAB)):
            arrived(("xw", way, i))
            start(("fw", way, i), W.at[pl.ds(base + i * PIECE, PIECE)],
                  W.at[pl.ds(base + LAB // 2 + i * PIECE, PIECE)], partner)

    def first(z, y, x, core):
        b, c = device(z, y, x, core)
        return (b * 8 + c) * LAB

    left, right = (x + XN - 1) % XN, (x + 1) % XN
    half = LAB // 2
    pieces = [
        (0, LAB, first(z, y, x, core)),
        (LAB, LAB, first(z, y, x, 1 - core)),
        (2 * LAB, half, first(z, y, left, core) + half),
        (2 * LAB + half, half, first(z, y, left, 1 - core) + half),
        (3 * LAB, half, first(z, y, right, core)),
        (3 * LAB + half, half, first(z, y, right, 1 - core)),
    ]

    def build_mask(slot):
        ids = IDS[slot]
        row = jnp.full(ids.shape, -1, jnp.int32)
        for base, count, label in pieces:
            local = ids - label
            row = jnp.where((local >= 0) & (local < count), local + base, row)
        low = jnp.where(row >= 0, row % 128, -1)
        bit = jnp.left_shift(1, jnp.maximum(row, 0) // 128)
        sub = lax.broadcasted_iota(jnp.int32, (128, QB), 0)
        m = jnp.zeros((128, QB), jnp.int32)
        for j in range(LIST):
            m = m | jnp.where(low[j:j + 1] == sub, bit[j:j + 1], 0)
        M[PLACE[slot] * QB:(PLACE[slot] + 1) * QB] = jnp.transpose(m)

    seen = set()

    def work(slot, part):
        at = PLACE[slot] * QB
        here, there = slice(at, at + 2 * QB), slice(part * 2 * LAB, (part + 1) * 2 * LAB)
        q, w, m = Q[here], W[there], M[here]
        scores = dot(q, w, NT)
        out = []
        for b in range(2 * LAB // 128):
            target = ((m >> (part * 2 * LAB // 128 + b)) & 1).astype(F32)
            out.append(((jax.nn.sigmoid(scores[:, b * 128:(b + 1) * 128]) - target) * loss_scale).astype(BF16))
        grad = jnp.concatenate(out, axis=1)
        a = dot(grad, w, NN)
        if (slot,) not in seen:
            QG[here] = a
        else:
            QG[here] += a
        g = dot(grad, q, TN)
        if part not in seen:
            WG[there] = g
        else:
            WG[there] += g
        seen.update([part, (slot,)])

    def reduce_y(slot):
        for k in range(PARTS[slot]):
            if slot == 4:
                there = (y + k + 1) % YN
                YS[slot, k] = QG[rows(slot, there % 2, there // 2)].astype(BF16)
                start(("yr", slot, k), YS.at[slot, k], YR.at[slot, k], y_of[k + 1])
            else:
                YS[slot, k] = QG[rows(slot, 1 - p, k)].astype(BF16)
                start(("yr", slot, k), YS.at[slot, k], YR.at[slot, k], y_of[3 - 2 * k])

    def eighth(which):
        return pl.ds(pl.multiple_of(which * (QB // 8), QB // 8), QB // 8)

    def total(slot, k):
        arrived(("yr", slot, k))
        t = QG[rows(slot, p, k)] + YR[slot, k].astype(F32)
        before = {2: 3, 1: 2, 6: 5, 7: 6}.get(slot)
        if before:
            arrived(("zr", before, k))
            t = t + ZR[slot, k].astype(F32)
        return t

    def reduce_z(slot):
        for k in range(2):
            ZS[slot, k] = total(slot, k).astype(BF16)
            start(("zr", slot, k), ZS.at[slot, k], ZR.at[TOWARDS[slot], k], z_of[1 if slot < 4 else 7])

    def reduce_last(slot):
        if slot == 4:
            arrived(*[("yr", 4, k) for k in range(3)])
            t = QG[rows(4, p, s)]
            for k in range(3):
                t = t + YR[4, k].astype(F32)
            LS[4, :QUARTER] = t.astype(BF16)
        else:
            for k in range(2):
                t = total(slot, k)
                LS[slot, k * QUARTER:(k + 1) * QUARTER] = t.astype(BF16)
                if slot == 0:
                    OWN[k * QUARTER:(k + 1) * QUARTER] = t
        for m in (3, 2, 1, 0):
            if ("zl", slot, m) in NAMES:
                j = (xh + m) % 2
                part = eighth(j if slot == 4 else (s + m // 2) % 2 * 2 + j)
                start(("zl", slot, m), LS.at[slot, part], LR.at[slot, m], owner(slot, m))

    cq.wait()
    pl.semaphore_wait(barrier, len(greeted))
    for slot in (7, 1):
        gather_z(slot, 0, 0)
    ci.wait()
    gather_ids(1)
    gather_ids(7)
    start(("id", 4), IDS.at[0], IDS.at[4], z_of[4])
    cw.wait()
    W[:LAB] = WF[...].astype(BF16)
    for slot in (7, 1):
        gather_z(slot, 1, 0)
    start(("cw",), W.at[pl.ds(0, LAB)], W.at[pl.ds(LAB, LAB)], partner)
    for i in range(SUB):
        start(("xw", "+", i), W.at[pl.ds(half + i * PIECE, PIECE)], W.at[pl.ds(2 * LAB + i * PIECE, PIECE)], x_of["+"])
        start(("xw", "-", i), W.at[pl.ds(i * PIECE, PIECE)], W.at[pl.ds(3 * LAB + i * PIECE, PIECE)], x_of["-"])
    build_mask(0)
    gather_step(1, 0)
    gather_ids(2)
    gather_ids(6)
    gather_step(1, 1)
    build_mask(1)
    build_mask(7)
    gather_step(2, 0)
    forward_weights(0)
    gather_ids(3)
    gather_ids(5)
    gather_step(2, 1)
    arrived(("cw",))
    gathered(1, 7)
    work(1, 0)
    gather_step(3, 0)
    forward_weights(1)
    build_mask(2)
    build_mask(6)
    gather_step(3, 1)
    gathered(2, 6)
    work(2, 0)
    forward_weights(2)
    forward_weights(3)
    arrived(("id", 4), ("id", 3), ("id", 5))
    build_mask(3)
    build_mask(5)
    gather_step(4, 0)
    gather_step(4, 1)
    build_mask(4)
    gathered(3, 5)
    work(3, 0)
    arrived(*[("fw", way, i) for way in "+-" for i in range(SUB)])
    work(3, 1)
    reduce_y(3)
    reduce_y(5)
    work(2, 1)
    reduce_y(2)
    reduce_y(6)
    gathered(4)
    work(4, 0)
    reduce_z(3)
    reduce_z(5)
    work(4, 1)
    reduce_y(4)
    reduce_y(0)
    work(1, 1)
    reduce_y(1)
    reduce_y(7)
    reduce_z(2)
    reduce_z(6)
    reduce_last(4)
    reduce_last(0)
    for n, (way, base) in enumerate((("+", 2 * LAB), ("-", 3 * LAB))):
        for i in range(SUB):
            GCS[n, i] = WG[base + half + i * PIECE:base + half + (i + 1) * PIECE].astype(BF16)
            start(("gc", way, i), GCS.at[n, i], GCR.at[n, i], partner)
    for i in range(SUB):
        for n, (way, base) in enumerate((("+", 2 * LAB), ("-", 3 * LAB))):
            arrived(("gc", way, i))
            GXS[n, i] = (WG[base + i * PIECE:base + (i + 1) * PIECE] + GCR[n, i].astype(F32)).astype(BF16)
            start(("gx", way, i), GXS.at[n, i], GXR.at[n, i], x_of["-" if way == "+" else "+"])
    for i in range(2):
        GOS[i] = WG[LAB + i * half:LAB + (i + 1) * half].astype(BF16)
        start(("go", i), GOS.at[i], GOR.at[i], partner)
    reduce_last(1)
    reduce_last(7)
    for i in range(2):
        arrived(("go", i))
        WG[i * half:(i + 1) * half] += GOR[i].astype(F32)

    t = OWN[eighth(s * 2 + xh)]
    for slot in (4, 0, 1, 7):
        for m in range(4):
            if ("zl", slot, m) in NAMES:
                arrived(("zl", slot, m))
                t = t + LR[slot, m].astype(F32)
    place = eighth(p * 4 + s * 2 + xh)
    OUT[place] = t.astype(BF16)
    for k in (5, 3, 7, 4, 1, 2, 6):
        start(("ag", k), OUT.at[place], OUT.at[place], same[k])
    for i in range(SUB):
        for n, (way, base) in enumerate((("+", half), ("-", 0))):
            arrived(("gx", way, i))
            wg_out[base + i * PIECE:base + (i + 1) * PIECE] = (
                WG[base + i * PIECE:base + (i + 1) * PIECE] + GXR[n, i].astype(F32)
            )
    sent(*[kind for kind in KINDS if kind != "ag"])
    arrived(("ag", 1))
    qg_out[...] = OUT[...]
    sent("ag")


def step(queries, label_ids, weights):
    vmem = pl.BlockSpec(memory_space=pltpu.VMEM)
    hbm = pl.BlockSpec(memory_space=pltpu.HBM)
    tokens = ZN * QB
    labels = 4 * LAB
    return pl.pallas_call(
        kernel,
        out_shape=(jax.ShapeDtypeStruct((LAB, D), F32), jax.ShapeDtypeStruct((QB, D), BF16)),
        in_specs=[hbm, hbm, hbm],
        out_specs=(vmem, vmem),
        scratch_shapes=[
            pltpu.VMEM((tokens, D), BF16),
            pltpu.VMEM((8, LIST, QB), jnp.int32),
            pltpu.VMEM((tokens, 128), jnp.int32),
            pltpu.VMEM((LAB, D), F32),
            pltpu.VMEM((labels, D), BF16),
            pltpu.VMEM((labels, D), F32),
            pltpu.VMEM((tokens, D), F32),
            pltpu.VMEM((8, 3, QUARTER, D), BF16),
            pltpu.VMEM((8, 3, QUARTER, D), BF16),
            pltpu.VMEM((8, 2, QUARTER, D), BF16),
            pltpu.VMEM((8, 2, QUARTER, D), BF16),
            pltpu.VMEM((2, LAB // 2, D), BF16),
            pltpu.VMEM((2, LAB // 2, D), BF16),
            pltpu.VMEM((2, SUB, PIECE, D), BF16),
            pltpu.VMEM((2, SUB, PIECE, D), BF16),
            pltpu.VMEM((2, SUB, PIECE, D), BF16),
            pltpu.VMEM((2, SUB, PIECE, D), BF16),
            pltpu.VMEM((8, QB // 2, D), BF16),
            pltpu.VMEM((8, 4, QB // 8, D), BF16),
            pltpu.VMEM((QB // 2, D), F32),
            pltpu.VMEM((QB, D), BF16),
            pltpu.SemaphoreType.DMA((3,)),
            pltpu.SemaphoreType.DMA((len(KINDS),)),
            pltpu.SemaphoreType.DMA((len(GROUPS),)),
        ],
        compiler_params=pltpu.CompilerParams(
            collective_id=0, has_side_effects=True, vmem_limit_bytes=40 * 1024 * 1024
        ),
        name="step",
    )(queries, label_ids, weights)


def body(queries, label_ids, weights, momentum):
    w_grad, q_grad = step(queries, label_ids.T, weights)
    new_momentum = keep_rate * momentum + w_grad
    new_weights = weights - step_rate * new_momentum
    return new_weights, new_momentum, q_grad.astype(F32)


def solution(mesh):
    return jax.shard_map(
        body,
        mesh=mesh,
        in_specs=(P("blk", None), P("blk", None), P(("blk", "cols"), None), P(("blk", "cols"), None)),
        out_specs=(P(("blk", "cols"), None), P(("blk", "cols"), None), P("blk", None)),
        check_vma=False,
    )
```

```python
import functools

import jax
import jax.numpy as jnp
from jax import lax
from jax.experimental import pallas as pl
from jax.experimental.pallas import tpu as pltpu
from jax.sharding import PartitionSpec as P

MESH = pl.DeviceIdType.MESH
F32, BF16 = jnp.float32, jnp.bfloat16
NT = (((1,), (1,)), ((), ()))
TN = (((0,), (0,)), ((), ()))
NN = (((1,), (0,)), ((), ()))

loss_scale = 1.0 / 16.0
keep_rate = 0.9
step_rate = 0.005

D = 768
LAB = 512
QB = 128
ZN, YN, XN = 8, 4, 4
LIST = 8
SUB = 4
PIECE = LAB // 2 // SUB
PLACE = {1: 0, 7: 1, 2: 2, 6: 3, 3: 4, 5: 5, 4: 6, 0: 7}
QUARTER = QB // 4


def dot(a, b, dims):
    return lax.dot_general(a, b, dims, preferred_element_type=F32)


def device(z, y, x, core):
    return (z * 4 + (x % 2) * 2 + core, y * 2 + x // 2)


TOWARDS = {3: 2, 2: 1, 1: 0, 5: 6, 6: 7, 7: 0}
PARTS = {slot: 3 if slot == 4 else 2 for slot in range(8)}


def copy_names():
    names = [("zg", r, k) for r in range(1, 8) for k in range(2)] + [("id", r) for r in range(1, 8)]
    names += [("yg", r, k) for r in range(1, 8) for k in range(2)]
    names += [("cw",)]
    names += [(kind, way, i) for kind in ("xw", "fw", "gc", "gx") for way in "+-" for i in range(SUB)]
    names += [("go", i) for i in range(2)]
    names += [("yr", r, k) for r in range(8) for k in range(PARTS[r])]
    names += [("zr", r, k) for r in (3, 2, 5, 6) for k in range(2)]
    names += [("zl", r, m) for r in (0, 1, 7, 4) for m in range(2 if r == 4 else 4) if r or m]
    names += [("ag", k) for k in range(1, 8)]
    return names


NAMES = copy_names()
ROWS = {"zg": QUARTER, "yg": QUARTER, "cw": LAB, "xw": PIECE, "fw": PIECE, "gc": PIECE, "gx": PIECE, "go": LAB // 2,
        "yr": QUARTER, "zr": QUARTER, "zl": QB // 8, "ag": QB // 8, "id": 0}


def group(name):
    if name[0] in ("fw", "ag"):
        return name[:1]
    if name[0] in ("yg", "zl") or name[:2] == ("yr", 4):
        return name[:2]
    return name


GROUPS = list(dict.fromkeys(group(name) for name in NAMES))
KINDS = list(ROWS)


def kernel(
    q_in, ids_in, w_in, wg_out, qg_out,
    Q, IDS, M, WF, W, WG, QG, YS, YR, ZS, ZR, GOS, GOR, GCS, GCR, GXS, GXR, LS, LR, OWN, OUT, local_sem, send_sem, recv_sem,
):
    blk, cols = lax.axis_index("blk"), lax.axis_index("cols")
    z, xl, core = blk // 4, (blk // 2) % 2, blk % 2
    y, xh = cols // 2, cols % 2
    x = xh * 2 + xl
    p = y % 2

    s = y // 2
    z_of = {r: device((z + r) % ZN, y, x, core) for r in range(1, 8)}
    y_of = {k: device(z, (y + k) % YN, x, core) for k in (1, 2, 3)}
    x_of = {"+": device(z, y, (x + 1) % XN, core), "-": device(z, y, (x + XN - 1) % XN, core)}
    partner = device(z, y, x, 1 - core)
    far_x = (x + 2) % XN
    same = {k: device(z, (y + k // 2) % YN, far_x if k % 2 else x, core) for k in range(1, 8)}

    cq = pltpu.make_async_copy(q_in, Q.at[pl.ds(PLACE[0] * QB, QB)], local_sem.at[0])
    cq.start()
    ci = pltpu.make_async_copy(ids_in, IDS.at[0], local_sem.at[2])
    ci.start()
    cw = pltpu.make_async_copy(w_in, WF, local_sem.at[1])
    cw.start()

    barrier = pltpu.get_barrier_semaphore()
    def owner(r, m):
        return device((z + r) % ZN, (y + 2 * (m // 2)) % YN, far_x if m % 2 else x, core)

    greeted = [partner] + list(x_of.values()) + list(same.values())
    greeted += [owner(r, m) for r in (1, 7) for m in range(4)] + [owner(4, 0), owner(4, 1)]
    for d in greeted:
        pl.semaphore_signal(barrier, inc=1, device_id=d, device_id_type=MESH)


    started, waited = [], set()

    def start(name, src, dst, dev):
        pltpu.make_async_remote_copy(
            src_ref=src, dst_ref=dst, send_sem=send_sem.at[KINDS.index(name[0])],
            recv_sem=recv_sem.at[GROUPS.index(group(name))], device_id=dev, device_id_type=MESH,
        ).start()
        started.append(name)

    def await_bytes(names, index, sent):
        if names[0][0] == "id":
            ref = IDS.at[pl.ds(0, len(names))]
        else:
            ref = W.at[pl.ds(0, sum(ROWS[name[0]] for name in names))]
        cp = pltpu.make_async_remote_copy(
            src_ref=ref, dst_ref=ref, send_sem=send_sem.at[index if sent else 0], recv_sem=recv_sem.at[0 if sent else index],
            device_id=partner, device_id_type=MESH,
        )
        if sent:
            cp.wait_send()
        else:
            cp.wait_recv()

    def arrived(*names):
        for key in dict.fromkeys(group(name) for name in names):
            if key not in waited:
                waited.add(key)
                await_bytes([name for name in NAMES if group(name) == key], GROUPS.index(key), False)

    def sent(*kinds):
        for kind in kinds:
            await_bytes([name for name in started if name[0] == kind], KINDS.index(kind), True)

    def rows(slot, half, quarter, count=QUARTER):
        return pl.ds(pl.multiple_of(PLACE[slot] * QB + half * (QB // 2) + quarter * QUARTER, QUARTER), count)

    def gather_z(slot, k, src):
        start(("zg", slot, k), Q.at[rows(src, p, k)], Q.at[rows(slot, p, k)], z_of[7 if src < 4 and slot == src + 1 else 1])

    def gather_ids(slot):
        src = TOWARDS[slot]
        if src:
            arrived(("id", src))
        start(("id", slot), IDS.at[src], IDS.at[slot], z_of[7 if slot < 4 else 1])

    def gather_step(step, k):
        for slot in (8 - step, step) if step < 4 else (4,):
            arrived(("zg", slot, k))
            if step < 3:
                gather_z(slot - 1 if slot > 4 else slot + 1, k, slot)
            elif step == 3 and slot == (5, 3)[k]:
                gather_z(4, k, slot)
            here = Q.at[rows(slot, p, k)]
            start(("yg", slot, k), here, here, y_of[1 + 2 * k])

    def gathered(*slots):
        for slot in slots:
            arrived(("yg", slot, 0), ("yg", slot, 1))

    def forward_weights(i):
        for way, base in (("+", 2 * LAB), ("-", 3 * LAB)):
            arrived(("xw", way, i))
            start(("fw", way, i), W.at[pl.ds(base + i * PIECE, PIECE)],
                  W.at[pl.ds(base + LAB // 2 + i * PIECE, PIECE)], partner)

    def first(z, y, x, core):
        b, c = device(z, y, x, core)
        return (b * 8 + c) * LAB

    left, right = (x + XN - 1) % XN, (x + 1) % XN
    half = LAB // 2
    pieces = [
        (0, LAB, first(z, y, x, core)),
        (LAB, LAB, first(z, y, x, 1 - core)),
        (2 * LAB, half, first(z, y, left, core) + half),
        (2 * LAB + half, half, first(z, y, left, 1 - core) + half),
        (3 * LAB, half, first(z, y, right, core)),
        (3 * LAB + half, half, first(z, y, right, 1 - core)),
    ]

    def build_mask(slot):
        ids = IDS[slot]
        row = jnp.full(ids.shape, -1, jnp.int32)
        for base, count, label in pieces:
            local = ids - label
            row = jnp.where((local >= 0) & (local < count), local + base, row)
        low = jnp.where(row >= 0, row % 128, -1)
        bit = jnp.left_shift(1, jnp.maximum(row, 0) // 128)
        sub = lax.broadcasted_iota(jnp.int32, (128, QB), 0)
        m = jnp.zeros((128, QB), jnp.int32)
        for j in range(LIST):
            m = m | jnp.where(low[j:j + 1] == sub, bit[j:j + 1], 0)
        M[PLACE[slot] * QB:(PLACE[slot] + 1) * QB] = jnp.transpose(m)

    seen = set()

    def work(slot, part):
        at = PLACE[slot] * QB
        here, there = slice(at, at + 2 * QB), slice(part * 2 * LAB, (part + 1) * 2 * LAB)
        q, w, m = Q[here], W[there], M[here]
        scores = dot(q, w, NT)
        out = []
        for b in range(2 * LAB // 128):
            target = ((m >> (part * 2 * LAB // 128 + b)) & 1).astype(F32)
            out.append(((jax.nn.sigmoid(scores[:, b * 128:(b + 1) * 128]) - target) * loss_scale).astype(BF16))
        grad = jnp.concatenate(out, axis=1)
        a = dot(grad, w, NN)
        if (slot,) not in seen:
            QG[here] = a
        else:
            QG[here] += a
        g = dot(grad, q, TN)
        if part not in seen:
            WG[there] = g
        else:
            WG[there] += g
        seen.update([part, (slot,)])

    def reduce_y(slot):
        for k in range(PARTS[slot]):
            if slot == 4:
                there = (y + k + 1) % YN
                YS[slot, k] = QG[rows(slot, there % 2, there // 2)].astype(BF16)
                start(("yr", slot, k), YS.at[slot, k], YR.at[slot, k], y_of[k + 1])
            else:
                YS[slot, k] = QG[rows(slot, 1 - p, k)].astype(BF16)
                start(("yr", slot, k), YS.at[slot, k], YR.at[slot, k], y_of[3 - 2 * k])

    def eighth(which):
        return pl.ds(pl.multiple_of(which * (QB // 8), QB // 8), QB // 8)

    def total(slot, k):
        arrived(("yr", slot, k))
        t = QG[rows(slot, p, k)] + YR[slot, k].astype(F32)
        before = {2: 3, 1: 2, 6: 5, 7: 6}.get(slot)
        if before:
            arrived(("zr", before, k))
            t = t + ZR[slot, k].astype(F32)
        return t

    def reduce_z(slot):
        for k in range(2):
            ZS[slot, k] = total(slot, k).astype(BF16)
            start(("zr", slot, k), ZS.at[slot, k], ZR.at[TOWARDS[slot], k], z_of[1 if slot < 4 else 7])

    def reduce_last(slot):
        if slot == 4:
            arrived(*[("yr", 4, k) for k in range(3)])
            t = QG[rows(4, p, s)]
            for k in range(3):
                t = t + YR[4, k].astype(F32)
            LS[4, :QUARTER] = t.astype(BF16)
        else:
            for k in range(2):
                t = total(slot, k)
                LS[slot, k * QUARTER:(k + 1) * QUARTER] = t.astype(BF16)
                if slot == 0:
                    OWN[k * QUARTER:(k + 1) * QUARTER] = t
        for m in (3, 2, 1, 0):
            if ("zl", slot, m) in NAMES:
                j = (xh + m) % 2
                part = eighth(j if slot == 4 else (s + m // 2) % 2 * 2 + j)
                start(("zl", slot, m), LS.at[slot, part], LR.at[slot, m], owner(slot, m))

    cq.wait()
    pl.semaphore_wait(barrier, len(greeted))
    for slot in (7, 1):
        gather_z(slot, 0, 0)
    ci.wait()
    gather_ids(1)
    gather_ids(7)
    start(("id", 4), IDS.at[0], IDS.at[4], z_of[4])
    cw.wait()
    W[:LAB] = WF[...].astype(BF16)
    for slot in (7, 1):
        gather_z(slot, 1, 0)
    start(("cw",), W.at[pl.ds(0, LAB)], W.at[pl.ds(LAB, LAB)], partner)
    for i in range(SUB):
        start(("xw", "+", i), W.at[pl.ds(half + i * PIECE, PIECE)], W.at[pl.ds(2 * LAB + i * PIECE, PIECE)], x_of["+"])
        start(("xw", "-", i), W.at[pl.ds(i * PIECE, PIECE)], W.at[pl.ds(3 * LAB + i * PIECE, PIECE)], x_of["-"])
    build_mask(0)
    gather_step(1, 0)
    gather_ids(2)
    gather_ids(6)
    gather_step(1, 1)
    build_mask(1)
    build_mask(7)
    gather_step(2, 0)
    forward_weights(0)
    gather_ids(3)
    gather_ids(5)
    gather_step(2, 1)
    arrived(("cw",))
    gathered(1, 7)
    work(1, 0)
    gather_step(3, 0)
    forward_weights(1)
    build_mask(2)
    build_mask(6)
    gather_step(3, 1)
    gathered(2, 6)
    work(2, 0)
    forward_weights(2)
    forward_weights(3)
    arrived(("id", 4), ("id", 3), ("id", 5))
    build_mask(3)
    build_mask(5)
    gather_step(4, 0)
    gather_step(4, 1)
    build_mask(4)
    gathered(3, 5)
    work(3, 0)
    arrived(*[("fw", way, i) for way in "+-" for i in range(SUB)])
    work(3, 1)
    reduce_y(3)
    reduce_y(5)
    work(2, 1)
    reduce_y(2)
    reduce_y(6)
    gathered(4)
    work(4, 0)
    reduce_z(3)
    reduce_z(5)
    work(4, 1)
    reduce_y(4)
    reduce_y(0)
    work(1, 1)
    reduce_y(1)
    reduce_y(7)
    for n, (way, base) in enumerate((("+", 2 * LAB), ("-", 3 * LAB))):
        for i in range(SUB):
            GCS[n, i] = WG[base + half + i * PIECE:base + half + (i + 1) * PIECE].astype(BF16)
            start(("gc", way, i), GCS.at[n, i], GCR.at[n, i], partner)
    reduce_z(2)
    reduce_z(6)
    reduce_last(4)
    reduce_last(0)
    for i in range(SUB):
        for n, (way, base) in enumerate((("+", 2 * LAB), ("-", 3 * LAB))):
            arrived(("gc", way, i))
            GXS[n, i] = (WG[base + i * PIECE:base + (i + 1) * PIECE] + GCR[n, i].astype(F32)).astype(BF16)
            start(("gx", way, i), GXS.at[n, i], GXR.at[n, i], x_of["-" if way == "+" else "+"])
    for i in range(2):
        GOS[i] = WG[LAB + i * half:LAB + (i + 1) * half].astype(BF16)
        start(("go", i), GOS.at[i], GOR.at[i], partner)
    reduce_last(1)
    reduce_last(7)
    for i in range(2):
        arrived(("go", i))
        WG[i * half:(i + 1) * half] += GOR[i].astype(F32)

    t = OWN[eighth(s * 2 + xh)]
    for slot in (4, 0, 1, 7):
        for m in range(4):
            if ("zl", slot, m) in NAMES:
                arrived(("zl", slot, m))
                t = t + LR[slot, m].astype(F32)
    place = eighth(p * 4 + s * 2 + xh)
    OUT[place] = t.astype(BF16)
    for k in (5, 3, 7, 4, 1, 2, 6):
        start(("ag", k), OUT.at[place], OUT.at[place], same[k])
    for i in range(SUB):
        for n, (way, base) in enumerate((("+", half), ("-", 0))):
            arrived(("gx", way, i))
            wg_out[base + i * PIECE:base + (i + 1) * PIECE] = (
                WG[base + i * PIECE:base + (i + 1) * PIECE] + GXR[n, i].astype(F32)
            )
    sent(*[kind for kind in KINDS if kind != "ag"])
    arrived(("ag", 1))
    qg_out[...] = OUT[...]
    sent("ag")


def step(queries, label_ids, weights):
    vmem = pl.BlockSpec(memory_space=pltpu.VMEM)
    hbm = pl.BlockSpec(memory_space=pltpu.HBM)
    tokens = ZN * QB
    labels = 4 * LAB
    return pl.pallas_call(
        kernel,
        out_shape=(jax.ShapeDtypeStruct((LAB, D), F32), jax.ShapeDtypeStruct((QB, D), BF16)),
        in_specs=[hbm, hbm, hbm],
        out_specs=(vmem, vmem),
        scratch_shapes=[
            pltpu.VMEM((tokens, D), BF16),
            pltpu.VMEM((8, LIST, QB), jnp.int32),
            pltpu.VMEM((tokens, 128), jnp.int32),
            pltpu.VMEM((LAB, D), F32),
            pltpu.VMEM((labels, D), BF16),
            pltpu.VMEM((labels, D), F32),
            pltpu.VMEM((tokens, D), F32),
            pltpu.VMEM((8, 3, QUARTER, D), BF16),
            pltpu.VMEM((8, 3, QUARTER, D), BF16),
            pltpu.VMEM((8, 2, QUARTER, D), BF16),
            pltpu.VMEM((8, 2, QUARTER, D), BF16),
            pltpu.VMEM((2, LAB // 2, D), BF16),
            pltpu.VMEM((2, LAB // 2, D), BF16),
            pltpu.VMEM((2, SUB, PIECE, D), BF16),
            pltpu.VMEM((2, SUB, PIECE, D), BF16),
            pltpu.VMEM((2, SUB, PIECE, D), BF16),
            pltpu.VMEM((2, SUB, PIECE, D), BF16),
            pltpu.VMEM((8, QB // 2, D), BF16),
            pltpu.VMEM((8, 4, QB // 8, D), BF16),
            pltpu.VMEM((QB // 2, D), F32),
            pltpu.VMEM((QB, D), BF16),
            pltpu.SemaphoreType.DMA((3,)),
            pltpu.SemaphoreType.DMA((len(KINDS),)),
            pltpu.SemaphoreType.DMA((len(GROUPS),)),
        ],
        compiler_params=pltpu.CompilerParams(
            collective_id=0, has_side_effects=True, vmem_limit_bytes=40 * 1024 * 1024
        ),
        name="step",
    )(queries, label_ids, weights)


def body(queries, label_ids, weights, momentum):
    w_grad, q_grad = step(queries, label_ids.T, weights)
    new_momentum = keep_rate * momentum + w_grad
    new_weights = weights - step_rate * new_momentum
    return new_weights, new_momentum, q_grad.astype(F32)


def solution(mesh):
    return jax.shard_map(
        body,
        mesh=mesh,
        in_specs=(P("blk", None), P("blk", None), P(("blk", "cols"), None), P(("blk", "cols"), None)),
        out_specs=(P(("blk", "cols"), None), P(("blk", "cols"), None), P("blk", None)),
        check_vma=False,
    )
```

```python
import functools

import jax
import jax.numpy as jnp
from jax import lax
from jax.experimental import pallas as pl
from jax.experimental.pallas import tpu as pltpu
from jax.sharding import PartitionSpec as P

MESH = pl.DeviceIdType.MESH
F32, BF16 = jnp.float32, jnp.bfloat16
NT = (((1,), (1,)), ((), ()))
TN = (((0,), (0,)), ((), ()))
NN = (((1,), (0,)), ((), ()))

loss_scale = 1.0 / 16.0
keep_rate = 0.9
step_rate = 0.005

D = 768
LAB = 512
QB = 128
ZN, YN, XN = 8, 4, 4
LIST = 8
SUB = 4
PIECE = LAB // 2 // SUB
PLACE = {1: 0, 7: 1, 2: 2, 6: 3, 3: 4, 5: 5, 4: 6, 0: 7}
QUARTER = QB // 4


def dot(a, b, dims):
    return lax.dot_general(a, b, dims, preferred_element_type=F32)


def device(z, y, x, core):
    return (z * 4 + (x % 2) * 2 + core, y * 2 + x // 2)


TOWARDS = {3: 2, 2: 1, 1: 0, 5: 6, 6: 7, 7: 0}
PARTS = {slot: 3 if slot == 4 else 2 for slot in range(8)}


def copy_names():
    names = [("zg", r, k) for r in range(1, 8) for k in range(2)] + [("id", r) for r in range(1, 8)]
    names += [("yg", r, k) for r in range(1, 8) for k in range(2)]
    names += [("cw",)]
    names += [(kind, way, i) for kind in ("xw", "fw", "gc", "gx") for way in "+-" for i in range(SUB)]
    names += [("go", i) for i in range(2)]
    names += [("yr", r, k) for r in range(8) for k in range(PARTS[r])]
    names += [("zr", r, k) for r in (3, 2, 5, 6) for k in range(2)]
    names += [("zl", r, m) for r in (0, 1, 7, 4) for m in range(2 if r == 4 else 4) if r or m]
    names += [("ag", k) for k in range(1, 8)]
    return names


NAMES = copy_names()
ROWS = {"zg": QUARTER, "yg": QUARTER, "cw": LAB, "xw": PIECE, "fw": PIECE, "gc": PIECE, "gx": PIECE, "go": LAB // 2,
        "yr": QUARTER, "zr": QUARTER, "zl": QB // 8, "ag": QB // 8, "id": 0}


def group(name):
    if name[0] in ("fw", "ag"):
        return name[:1]
    if name[0] in ("yg", "zl") or name[:2] == ("yr", 4):
        return name[:2]
    return name


GROUPS = list(dict.fromkeys(group(name) for name in NAMES))
KINDS = list(ROWS)


def kernel(
    q_in, ids_in, w_in, wg_out, qg_out,
    Q, IDS, M, WF, W, WG, QG, YS, YR, ZS, ZR, GOS, GOR, GCS, GCR, GXS, GXR, LS, LR, OWN, OUT, local_sem, send_sem, recv_sem,
):
    blk, cols = lax.axis_index("blk"), lax.axis_index("cols")
    z, xl, core = blk // 4, (blk // 2) % 2, blk % 2
    y, xh = cols // 2, cols % 2
    x = xh * 2 + xl
    p = y % 2

    s = y // 2
    z_of = {r: device((z + r) % ZN, y, x, core) for r in range(1, 8)}
    y_of = {k: device(z, (y + k) % YN, x, core) for k in (1, 2, 3)}
    x_of = {"+": device(z, y, (x + 1) % XN, core), "-": device(z, y, (x + XN - 1) % XN, core)}
    partner = device(z, y, x, 1 - core)
    far_x = (x + 2) % XN
    same = {k: device(z, (y + k // 2) % YN, far_x if k % 2 else x, core) for k in range(1, 8)}

    cq = pltpu.make_async_copy(q_in, Q.at[pl.ds(PLACE[0] * QB, QB)], local_sem.at[0])
    cq.start()
    ci = pltpu.make_async_copy(ids_in, IDS.at[0], local_sem.at[2])
    ci.start()
    cw = pltpu.make_async_copy(w_in, WF, local_sem.at[1])
    cw.start()

    barrier = pltpu.get_barrier_semaphore()
    def owner(r, m):
        return device((z + r) % ZN, (y + 2 * (m // 2)) % YN, far_x if m % 2 else x, core)

    greeted = [partner] + list(x_of.values()) + list(same.values())
    greeted += [owner(r, m) for r in (1, 7) for m in range(4)] + [owner(4, 0), owner(4, 1)]
    for d in greeted:
        pl.semaphore_signal(barrier, inc=1, device_id=d, device_id_type=MESH)


    started, waited = [], set()

    def start(name, src, dst, dev):
        pltpu.make_async_remote_copy(
            src_ref=src, dst_ref=dst, send_sem=send_sem.at[KINDS.index(name[0])],
            recv_sem=recv_sem.at[GROUPS.index(group(name))], device_id=dev, device_id_type=MESH,
        ).start()
        started.append(name)

    def await_bytes(names, index, sent):
        if names[0][0] == "id":
            ref = IDS.at[pl.ds(0, len(names))]
        else:
            ref = W.at[pl.ds(0, sum(ROWS[name[0]] for name in names))]
        cp = pltpu.make_async_remote_copy(
            src_ref=ref, dst_ref=ref, send_sem=send_sem.at[index if sent else 0], recv_sem=recv_sem.at[0 if sent else index],
            device_id=partner, device_id_type=MESH,
        )
        if sent:
            cp.wait_send()
        else:
            cp.wait_recv()

    def arrived(*names):
        for key in dict.fromkeys(group(name) for name in names):
            if key not in waited:
                waited.add(key)
                await_bytes([name for name in NAMES if group(name) == key], GROUPS.index(key), False)

    def sent(*kinds):
        for kind in kinds:
            await_bytes([name for name in started if name[0] == kind], KINDS.index(kind), True)

    def rows(slot, half, quarter, count=QUARTER):
        return pl.ds(pl.multiple_of(PLACE[slot] * QB + half * (QB // 2) + quarter * QUARTER, QUARTER), count)

    def gather_z(slot, k, src):
        start(("zg", slot, k), Q.at[rows(src, p, k)], Q.at[rows(slot, p, k)], z_of[7 if src < 4 and slot == src + 1 else 1])

    def gather_ids(slot):
        src = TOWARDS[slot]
        if src:
            arrived(("id", src))
        start(("id", slot), IDS.at[src], IDS.at[slot], z_of[7 if slot < 4 else 1])

    def gather_step(step, k):
        for slot in (8 - step, step) if step < 4 else (4,):
            arrived(("zg", slot, k))
            if step < 3:
                gather_z(slot - 1 if slot > 4 else slot + 1, k, slot)
            elif step == 3 and slot == (5, 3)[k]:
                gather_z(4, k, slot)
            here = Q.at[rows(slot, p, k)]
            start(("yg", slot, k), here, here, y_of[1 + 2 * k])

    def gathered(*slots):
        for slot in slots:
            arrived(("yg", slot, 0), ("yg", slot, 1))

    def forward_weights(i):
        for way, base in (("+", 2 * LAB), ("-", 3 * LAB)):
            arrived(("xw", way, i))
            start(("fw", way, i), W.at[pl.ds(base + i * PIECE, PIECE)],
                  W.at[pl.ds(base + LAB // 2 + i * PIECE, PIECE)], partner)

    def first(z, y, x, core):
        b, c = device(z, y, x, core)
        return (b * 8 + c) * LAB

    left, right = (x + XN - 1) % XN, (x + 1) % XN
    half = LAB // 2
    pieces = [
        (0, LAB, first(z, y, x, core)),
        (LAB, LAB, first(z, y, x, 1 - core)),
        (2 * LAB, half, first(z, y, left, core) + half),
        (2 * LAB + half, half, first(z, y, left, 1 - core) + half),
        (3 * LAB, half, first(z, y, right, core)),
        (3 * LAB + half, half, first(z, y, right, 1 - core)),
    ]

    def build_mask(slot):
        ids = IDS[slot]
        row = jnp.full(ids.shape, -1, jnp.int32)
        for base, count, label in pieces:
            local = ids - label
            row = jnp.where((local >= 0) & (local < count), local + base, row)
        low = jnp.where(row >= 0, row % 128, -1)
        bit = jnp.left_shift(1, jnp.maximum(row, 0) // 128)
        sub = lax.broadcasted_iota(jnp.int32, (128, QB), 0)
        m = jnp.zeros((128, QB), jnp.int32)
        for j in range(LIST):
            m = m | jnp.where(low[j:j + 1] == sub, bit[j:j + 1], 0)
        M[PLACE[slot] * QB:(PLACE[slot] + 1) * QB] = jnp.transpose(m)

    seen = set()

    def work(slot, part):
        at = PLACE[slot] * QB
        here, there = slice(at, at + 2 * QB), slice(part * 2 * LAB, (part + 1) * 2 * LAB)
        q, w, m = Q[here], W[there], M[here]
        scores = dot(q, w, NT)
        out = []
        for b in range(2 * LAB // 128):
            target = ((m >> (part * 2 * LAB // 128 + b)) & 1).astype(F32)
            out.append(((jax.nn.sigmoid(scores[:, b * 128:(b + 1) * 128]) - target) * loss_scale).astype(BF16))
        grad = jnp.concatenate(out, axis=1)
        a = dot(grad, w, NN)
        if (slot,) not in seen:
            QG[here] = a
        else:
            QG[here] += a
        g = dot(grad, q, TN)
        if part not in seen:
            WG[there] = g
        else:
            WG[there] += g
        seen.update([part, (slot,)])

    def reduce_y(slot):
        for k in range(PARTS[slot]):
            if slot == 4:
                there = (y + k + 1) % YN
                YS[slot, k] = QG[rows(slot, there % 2, there // 2)].astype(BF16)
                start(("yr", slot, k), YS.at[slot, k], YR.at[slot, k], y_of[k + 1])
            else:
                YS[slot, k] = QG[rows(slot, 1 - p, k)].astype(BF16)
                start(("yr", slot, k), YS.at[slot, k], YR.at[slot, k], y_of[3 - 2 * k])

    def eighth(which):
        return pl.ds(pl.multiple_of(which * (QB // 8), QB // 8), QB // 8)

    def total(slot, k):
        arrived(("yr", slot, k))
        t = QG[rows(slot, p, k)] + YR[slot, k].astype(F32)
        before = {2: 3, 1: 2, 6: 5, 7: 6}.get(slot)
        if before:
            arrived(("zr", before, k))
            t = t + ZR[slot, k].astype(F32)
        return t

    def reduce_z(slot):
        for k in range(2):
            ZS[slot, k] = total(slot, k).astype(BF16)
            start(("zr", slot, k), ZS.at[slot, k], ZR.at[TOWARDS[slot], k], z_of[1 if slot < 4 else 7])

    def reduce_last(slot):
        if slot == 4:
            arrived(*[("yr", 4, k) for k in range(3)])
            t = QG[rows(4, p, s)]
            for k in range(3):
                t = t + YR[4, k].astype(F32)
            LS[4, :QUARTER] = t.astype(BF16)
        else:
            for k in range(2):
                t = total(slot, k)
                LS[slot, k * QUARTER:(k + 1) * QUARTER] = t.astype(BF16)
                if slot == 0:
                    OWN[k * QUARTER:(k + 1) * QUARTER] = t
        for m in (3, 2, 1, 0):
            if ("zl", slot, m) in NAMES:
                j = (xh + m) % 2
                part = eighth(j if slot == 4 else (s + m // 2) % 2 * 2 + j)
                start(("zl", slot, m), LS.at[slot, part], LR.at[slot, m], owner(slot, m))

    cq.wait()
    pl.semaphore_wait(barrier, len(greeted))
    for slot in (7, 1):
        gather_z(slot, 0, 0)
    ci.wait()
    gather_ids(1)
    gather_ids(7)
    start(("id", 4), IDS.at[0], IDS.at[4], z_of[4])
    cw.wait()
    W[:LAB] = WF[...].astype(BF16)
    for slot in (7, 1):
        gather_z(slot, 1, 0)
    start(("cw",), W.at[pl.ds(0, LAB)], W.at[pl.ds(LAB, LAB)], partner)
    for i in range(SUB):
        start(("xw", "+", i), W.at[pl.ds(half + i * PIECE, PIECE)], W.at[pl.ds(2 * LAB + i * PIECE, PIECE)], x_of["+"])
        start(("xw", "-", i), W.at[pl.ds(i * PIECE, PIECE)], W.at[pl.ds(3 * LAB + i * PIECE, PIECE)], x_of["-"])
    build_mask(0)
    gather_step(1, 0)
    gather_ids(2)
    gather_ids(6)
    gather_step(1, 1)
    build_mask(1)
    build_mask(7)
    gather_step(2, 0)
    forward_weights(0)
    gather_ids(3)
    gather_ids(5)
    gather_step(2, 1)
    arrived(("cw",))
    gathered(1, 7)
    work(1, 0)
    gather_step(3, 0)
    forward_weights(1)
    build_mask(2)
    build_mask(6)
    gather_step(3, 1)
    gathered(2, 6)
    work(2, 0)
    forward_weights(2)
    forward_weights(3)
    arrived(("id", 4), ("id", 3), ("id", 5))
    build_mask(3)
    build_mask(5)
    gather_step(4, 0)
    gather_step(4, 1)
    build_mask(4)
    gathered(3, 5)
    work(3, 0)
    arrived(*[("fw", way, i) for way in "+-" for i in range(SUB)])
    work(3, 1)
    reduce_y(3)
    reduce_y(5)
    work(2, 1)
    reduce_y(2)
    reduce_y(6)
    gathered(4)
    work(4, 0)
    reduce_z(3)
    reduce_z(5)
    work(4, 1)
    reduce_y(4)
    reduce_y(0)
    work(1, 1)
    reduce_y(1)
    reduce_y(7)
    for n, (way, base) in enumerate((("+", 2 * LAB), ("-", 3 * LAB))):
        for i in range(SUB):
            GCS[n, i] = WG[base + half + i * PIECE:base + half + (i + 1) * PIECE].astype(BF16)
            start(("gc", way, i), GCS.at[n, i], GCR.at[n, i], partner)
    reduce_z(2)
    reduce_z(6)
    for i in range(SUB):
        for n, (way, base) in enumerate((("+", 2 * LAB), ("-", 3 * LAB))):
            arrived(("gc", way, i))
            GXS[n, i] = (WG[base + i * PIECE:base + (i + 1) * PIECE] + GCR[n, i].astype(F32)).astype(BF16)
            start(("gx", way, i), GXS.at[n, i], GXR.at[n, i], x_of["-" if way == "+" else "+"])
    reduce_last(4)
    reduce_last(0)
    for i in range(2):
        GOS[i] = WG[LAB + i * half:LAB + (i + 1) * half].astype(BF16)
        start(("go", i), GOS.at[i], GOR.at[i], partner)
    reduce_last(1)
    reduce_last(7)
    for i in range(2):
        arrived(("go", i))
        WG[i * half:(i + 1) * half] += GOR[i].astype(F32)

    t = OWN[eighth(s * 2 + xh)]
    for slot in (4, 0, 1, 7):
        for m in range(4):
            if ("zl", slot, m) in NAMES:
                arrived(("zl", slot, m))
                t = t + LR[slot, m].astype(F32)
    place = eighth(p * 4 + s * 2 + xh)
    OUT[place] = t.astype(BF16)
    for k in (5, 3, 7, 4, 1, 2, 6):
        start(("ag", k), OUT.at[place], OUT.at[place], same[k])
    for i in range(SUB):
        for n, (way, base) in enumerate((("+", half), ("-", 0))):
            arrived(("gx", way, i))
            wg_out[base + i * PIECE:base + (i + 1) * PIECE] = (
                WG[base + i * PIECE:base + (i + 1) * PIECE] + GXR[n, i].astype(F32)
            )
    sent(*[kind for kind in KINDS if kind != "ag"])
    arrived(("ag", 1))
    qg_out[...] = OUT[...]
    sent("ag")


def step(queries, label_ids, weights):
    vmem = pl.BlockSpec(memory_space=pltpu.VMEM)
    hbm = pl.BlockSpec(memory_space=pltpu.HBM)
    tokens = ZN * QB
    labels = 4 * LAB
    return pl.pallas_call(
        kernel,
        out_shape=(jax.ShapeDtypeStruct((LAB, D), F32), jax.ShapeDtypeStruct((QB, D), BF16)),
        in_specs=[hbm, hbm, hbm],
        out_specs=(vmem, vmem),
        scratch_shapes=[
            pltpu.VMEM((tokens, D), BF16),
            pltpu.VMEM((8, LIST, QB), jnp.int32),
            pltpu.VMEM((tokens, 128), jnp.int32),
            pltpu.VMEM((LAB, D), F32),
            pltpu.VMEM((labels, D), BF16),
            pltpu.VMEM((labels, D), F32),
            pltpu.VMEM((tokens, D), F32),
            pltpu.VMEM((8, 3, QUARTER, D), BF16),
            pltpu.VMEM((8, 3, QUARTER, D), BF16),
            pltpu.VMEM((8, 2, QUARTER, D), BF16),
            pltpu.VMEM((8, 2, QUARTER, D), BF16),
            pltpu.VMEM((2, LAB // 2, D), BF16),
            pltpu.VMEM((2, LAB // 2, D), BF16),
            pltpu.VMEM((2, SUB, PIECE, D), BF16),
            pltpu.VMEM((2, SUB, PIECE, D), BF16),
            pltpu.VMEM((2, SUB, PIECE, D), BF16),
            pltpu.VMEM((2, SUB, PIECE, D), BF16),
            pltpu.VMEM((8, QB // 2, D), BF16),
            pltpu.VMEM((8, 4, QB // 8, D), BF16),
            pltpu.VMEM((QB // 2, D), F32),
            pltpu.VMEM((QB, D), BF16),
            pltpu.SemaphoreType.DMA((3,)),
            pltpu.SemaphoreType.DMA((len(KINDS),)),
            pltpu.SemaphoreType.DMA((len(GROUPS),)),
        ],
        compiler_params=pltpu.CompilerParams(
            collective_id=0, has_side_effects=True, vmem_limit_bytes=40 * 1024 * 1024
        ),
        name="step",
    )(queries, label_ids, weights)


def body(queries, label_ids, weights, momentum):
    w_grad, q_grad = step(queries, label_ids.T, weights)
    new_momentum = keep_rate * momentum + w_grad
    new_weights = weights - step_rate * new_momentum
    return new_weights, new_momentum, q_grad.astype(F32)


def solution(mesh):
    return jax.shard_map(
        body,
        mesh=mesh,
        in_specs=(P("blk", None), P("blk", None), P(("blk", "cols"), None), P(("blk", "cols"), None)),
        out_specs=(P(("blk", "cols"), None), P(("blk", "cols"), None), P("blk", None)),
        check_vma=False,
    )
```
